1024 devices in a mesh: fsdp: 64 (over y, x), tensor: 16 (over z, core).
Axes of the slice: x: 8, y: 8, z: 8, core: 2. Of those that a mesh axis runs over, the one named last changes fastest.
Arguments:
- weight: float32 [4096, 14336], P('fsdp', 'tensor'), may hold values from -6 to 6
- momentum: float32 [4096, 14336], P('fsdp', 'tensor'), may hold values from -6 to 6
- gradient: bfloat16 [4096, 14336], P('fsdp', 'tensor'), may hold values from -90 to 90, as said below
- right_basis: float32 [14336, 64], P('tensor'), may hold values from -0.046875 to 0.046875
Outputs:
- new_weight: float32 [4096, 14336], P('fsdp', 'tensor')
- new_momentum: float32 [4096, 14336], P('fsdp', 'tensor')
- new_basis: float32 [14336, 64], P('tensor')
The draws below stay inside these ranges and needn't reach their ends.
Inputs may be any that keep to these rules, and one draw needn't show every extreme that they name: Entries of the gradient are real-valued with row and column scales that differ widely.
All inputs are finite; a program needn't handle non-finite values.
Results may differ from the reference program's by a relative error of at most 0.0004.
Values sent between devices are 32-bit elements; how exact they have to be, the bound alone decides.
No kernel may reach another device: no remote copies, remote signals or barrier semaphores. Data moves between devices by JAX's collectives and lax.ppermute only.
A program may use at most 32 MiB of HBM per device.

```python
import math
import jax
import jax.numpy as jnp
from jax import lax

ROWS = 4096
COLS = 14336
RANK = 64


def draw_gradient(key, part):
    key = jax.random.fold_in(key, 7)
    keys = jax.random.split(key, 5)
    row_ramp = 3.0 ** (jnp.arange(ROWS, dtype=jnp.float32) / (ROWS - 1))
    col_ramp = 3.0 ** (jnp.arange(COLS, dtype=jnp.float32) / (COLS - 1))
    row_scale = 10.0 ** jax.random.uniform(keys[0], (ROWS,), jnp.float32) * row_ramp
    col_scale = 10.0 ** jax.random.uniform(keys[1], (COLS,), jnp.float32) * col_ramp
    base = jnp.clip(jax.random.normal(keys[4], (ROWS, COLS), jnp.float32), -4.0, 4.0)
    return (base * row_scale[:, None] * col_scale[None, :] / 40.0).astype(jnp.bfloat16)


def block_levels(stream_key, dims, shards, smallest, high):
    def one(dim, blocks):
        heights = jax.random.uniform(jax.random.fold_in(jax.random.fold_in(stream_key, 6), dim), (blocks,), jnp.float32, smallest / len(shards), high / len(shards))
        return jnp.repeat(jnp.exp(heights), dims[dim] // blocks).reshape((-1,) + (1,) * (len(dims) - dim - 1))

    level = one(*shards[0])
    for cut in shards[1:]:
        level = level * one(*cut)
    return level


def centred(rng, extent, deviation, limit, pieces=(), kind=jnp.bfloat16):
    gain = block_levels(rng, extent, pieces, -0.22, 0.18) if pieces else 1.0
    array = jax.random.normal(rng, extent, jnp.float32) * deviation * gain
    return jnp.minimum(jnp.maximum(array, -limit), limit).astype(kind)


def setup_inputs(seed: int = 0) -> dict:
    arg_keys = jax.random.split(jax.random.key(seed), 5)
    weight = centred(arg_keys[0], (ROWS, COLS), 1.0, 6.0, ((0, 64), (1, 16)), jnp.float32)
    momentum = centred(arg_keys[1], (ROWS, COLS), 1.0, 6.0, ((0, 64), (1, 16)), jnp.float32)
    gradient = draw_gradient(jax.random.fold_in(arg_keys[4], 71), 0)
    right_basis = centred(arg_keys[3], (COLS, RANK), COLS ** -0.5, 0.046875, ((0, 16),), jnp.float32)
    return dict(weight=weight, momentum=momentum, gradient=gradient, right_basis=right_basis)


decay_rate = 0.95
step_size = 0.3
tiny_eps = 1e-08

def reference(weight, momentum, gradient, right_basis):
    highest = lax.Precision.HIGHEST
    buffer = momentum + gradient.astype(jnp.float32)
    left = jnp.dot(buffer, right_basis, precision=highest)
    gram_matrix = jnp.dot(left.T, left, precision=highest)
    lower_factor = jnp.linalg.cholesky(gram_matrix)
    ortho = jax.scipy.linalg.solve_triangular(lower_factor, left.T, lower=True).T
    right_factor = jnp.dot(buffer.T, ortho, precision=highest)
    norms = jnp.sqrt(lax.optimization_barrier(jnp.sum(right_factor * right_factor, axis=0)))
    new_basis = right_factor / (norms + tiny_eps)
    new_momentum = buffer - (1.0 - decay_rate) * jnp.dot(ortho, right_factor.T, precision=highest)
    factor = step_size * math.sqrt(ROWS * COLS / RANK)
    new_weight = weight - factor * jnp.dot(ortho, new_basis.T, precision=highest)
    return (new_weight, new_momentum, new_basis)
```

```python
import math

import jax
import jax.numpy as jnp
from jax import lax
from jax.sharding import PartitionSpec as P

decay_rate = 0.95
step_size = 0.3
tiny_eps = 1e-08


def exchange(blocks, axis):
    return lax.all_to_all(blocks, axis, 0, 0)


def sum_everywhere(block, axis):
    copies = jnp.broadcast_to(block[None], (lax.axis_size(axis),) + block.shape)
    return jnp.sum(exchange(copies, axis), axis=0)


def gather(block, axis):
    copies = jnp.broadcast_to(block[None], (lax.axis_size(axis),) + block.shape)
    return exchange(copies, axis)


def per_device(weight, momentum, gradient, right_basis):
    highest = lax.Precision.HIGHEST
    rank = right_basis.shape[1]
    rows, cols = weight.shape
    buffer = momentum + gradient.astype(jnp.float32)
    left_part = jnp.dot(buffer, right_basis, precision=highest)
    half = rows // 2
    packed = jnp.concatenate([left_part[:half], left_part[half:]], axis=1)
    packed = sum_everywhere(packed, "tensor")
    left = jnp.concatenate([packed[:, :rank], packed[:, rank:]], axis=0)
    wide = jnp.concatenate([buffer, left, jnp.zeros((rows, 1024 - cols - rank), jnp.float32)], axis=1)
    products = jnp.dot(left.T, wide, precision=highest).reshape(rank, 8, 128)
    mine = jnp.sum(exchange(products, "fsdp"), axis=0)
    whole = gather(mine, "fsdp").reshape(rank, 1024)
    gram_matrix = whole[:, cols:cols + rank]
    lower_factor = jnp.linalg.cholesky(gram_matrix)
    both = jnp.concatenate([whole[:, :cols], left.T], axis=1)
    both = jax.scipy.linalg.solve_triangular(lower_factor, both, lower=True)
    right_t = both[:, :cols]
    ortho = both[:, cols:].T
    right_factor = right_t.T
    squares = jnp.sum(right_factor * right_factor, axis=0)
    squares = jnp.broadcast_to(jnp.pad(squares, (0, 128 - rank))[None], (8, 128))
    norms = jnp.sqrt(sum_everywhere(squares, "tensor")[0, :rank])
    new_basis = right_factor / (norms + tiny_eps)
    new_momentum = buffer - (1.0 - decay_rate) * jnp.dot(ortho, right_t, precision=highest)
    total_rows = weight.shape[0] * lax.axis_size("fsdp")
    total_cols = weight.shape[1] * lax.axis_size("tensor")
    factor = step_size * math.sqrt(total_rows * total_cols / rank)
    new_weight = weight - factor * jnp.dot(ortho, new_basis.T, precision=highest)
    return (new_weight, new_momentum, new_basis)


def solution(mesh):
    placed = (P("fsdp", "tensor"), P("fsdp", "tensor"), P("fsdp", "tensor"), P("tensor", None))
    return jax.shard_map(
        per_device,
        mesh=mesh,
        in_specs=placed,
        out_specs=(P("fsdp", "tensor"), P("fsdp", "tensor"), P("tensor", None)),
        check_vma=False,
    )
```

```python
import math

import jax
import jax.numpy as jnp
from jax import lax
from jax.experimental import pallas as pl
from jax.experimental.pallas import tpu as pltpu
from jax.sharding import PartitionSpec as P

decay_rate = 0.95
step_size = 0.3
tiny_eps = 1e-08
highest = lax.Precision.HIGHEST
f32 = jnp.float32


def exchange(blocks, axis):
    return lax.all_to_all(blocks, axis, 0, 0)


def copies(block, axis):
    return jnp.broadcast_to(block[None], (lax.axis_size(axis),) + block.shape)


def eliminate(blocks, size, width):
    sublane = lax.broadcasted_iota(jnp.int32, (8, width), 0)

    def spread_row(block, row):
        return jnp.broadcast_to(block[row:row + 1, :], (8, width))

    def spread_column(block, column):
        return jnp.broadcast_to(block[:, column:column + 1], (8, width))

    count = size // 8
    for first in range(count):
        live = range(first, count)
        columns = [{i: spread_column(blocks[i], 8 * first + k) for i in live} for k in range(8)]
        for k in range(8):
            inverse = 1.0 / spread_row(columns[k][first], k)
            row = spread_row(blocks[first], k)
            ratio = {i: columns[k][i] * inverse for i in live}
            ratio[first] = jnp.where(sublane > k, ratio[first], 0.0)
            for later in range(k + 1, 8):
                entry = spread_row(columns[later][first], k)
                for i in live:
                    columns[later][i] = columns[later][i] - ratio[i] * entry
            for i in live:
                if i > first or k < 7:
                    blocks[i] = blocks[i] - ratio[i] * row
    return blocks


def factor_kernel(whole_ref, left_ref, right_ref, ortho_ref, squares_ref):
    rank = left_ref.shape[1]
    slabs = right_ref.shape[1] // 128
    row = lax.broadcasted_iota(jnp.int32, (rank, 2 * rank), 0)
    column = lax.broadcasted_iota(jnp.int32, (rank, 2 * rank), 1)
    start = jnp.where(column < rank, whole_ref[:, slabs, :], jnp.where(column == row + rank, 1.0, 0.0))
    blocks = eliminate([start[8 * i:8 * i + 8] for i in range(rank // 8)], rank, 2 * rank)
    done = jnp.concatenate(blocks, axis=0)
    pivots = jnp.sum(jnp.where(row == column, done, 0.0), axis=1, keepdims=True)
    inverse = (done / jnp.sqrt(pivots))[:, rank:]
    total = jnp.zeros((rank, 128), f32)
    for slab in range(slabs):
        right = jnp.dot(inverse, whole_ref[:, slab, :], precision=highest, preferred_element_type=f32)
        right_ref[:, 128 * slab:128 * slab + 128] = right
        total = total + right * right
    by_columns = (((1,), (1,)), ((), ()))
    ortho_ref[...] = lax.dot_general(left_ref[...], inverse, by_columns, precision=highest, preferred_element_type=f32)
    squares = lax.dot_general(jnp.ones((8, 128), f32), total, by_columns, precision=highest, preferred_element_type=f32)
    squares_ref[...] = jnp.concatenate([squares, jnp.zeros((8, 128 - rank), f32)], axis=1)


def per_device(weight, momentum, gradient, right_basis):
    rank = right_basis.shape[1]
    rows, cols = weight.shape
    buffer = momentum + gradient.astype(f32)
    left_part = jnp.dot(buffer, right_basis, precision=highest)
    half = rows // 2
    packed = jnp.concatenate([left_part[:half], left_part[half:]], axis=1)
    packed = jnp.sum(exchange(copies(packed, "tensor"), "tensor"), axis=0)
    left = jnp.concatenate([packed[:, :rank], packed[:, rank:]], axis=0)
    wide = jnp.concatenate([buffer, left, jnp.zeros((rows, 1024 - cols - rank), f32)], axis=1)
    products = jnp.dot(left.T, wide, precision=highest).reshape(rank, 8, 128)
    mine = jnp.sum(exchange(products, "fsdp"), axis=0)
    whole = exchange(copies(mine, "fsdp"), "fsdp")
    in_vmem = pl.BlockSpec(memory_space=pltpu.VMEM)
    right_t, ortho, squares = pl.pallas_call(
        factor_kernel,
        out_shape=[
            jax.ShapeDtypeStruct((rank, cols), f32),
            jax.ShapeDtypeStruct((rows, rank), f32),
            jax.ShapeDtypeStruct((8, 128), f32),
        ],
        in_specs=[in_vmem] * 2,
        out_specs=[in_vmem] * 3,
        name="factor",
    )(whole, left)
    squares = jnp.sum(exchange(copies(squares, "tensor"), "tensor"), axis=0)
    norms = jnp.sqrt(squares[0, :rank])
    new_basis = right_t.T / (norms + tiny_eps)
    new_momentum = buffer - (1.0 - decay_rate) * jnp.dot(ortho, right_t, precision=highest)
    total_rows = rows * lax.axis_size("fsdp")
    total_cols = cols * lax.axis_size("tensor")
    factor = step_size * math.sqrt(total_rows * total_cols / rank)
    new_weight = weight - factor * jnp.dot(ortho, new_basis.T, precision=highest)
    return (new_weight, new_momentum, new_basis)


def solution(mesh):
    placed = (P("fsdp", "tensor"), P("fsdp", "tensor"), P("fsdp", "tensor"), P("tensor", None))
    return jax.shard_map(
        per_device,
        mesh=mesh,
        in_specs=placed,
        out_specs=(P("fsdp", "tensor"), P("fsdp", "tensor"), P("tensor", None)),
        check_vma=False,
    )
```

```python
import functools
import math

import jax
import jax.numpy as jnp
from jax import lax
from jax.experimental import pallas as pl
from jax.experimental.pallas import tpu as pltpu
from jax.sharding import PartitionSpec as P

decay_rate = 0.95
step_size = 0.3
tiny_eps = 1e-08
highest = lax.Precision.HIGHEST
f32 = jnp.float32


def exchange(blocks, axis):
    return lax.all_to_all(blocks, axis, 0, 0)


def copies(block, axis):
    return jnp.broadcast_to(block[None], (lax.axis_size(axis),) + block.shape)


def eliminate(blocks, size, width):
    sublane = lax.broadcasted_iota(jnp.int32, (8, width), 0)

    def spread_row(block, row):
        return jnp.broadcast_to(block[row:row + 1, :], (8, width))

    def spread_column(block, column):
        return jnp.broadcast_to(block[:, column:column + 1], (8, width))

    count = size // 8
    for first in range(count):
        live = range(first, count)
        columns = [{i: spread_column(blocks[i], 8 * first + k) for i in live} for k in range(8)]
        for k in range(8):
            inverse = 1.0 / spread_row(columns[k][first], k)
            row = spread_row(blocks[first], k)
            ratio = {i: columns[k][i] * inverse for i in live}
            ratio[first] = jnp.where(sublane > k, ratio[first], 0.0)
            for later in range(k + 1, 8):
                entry = spread_row(columns[later][first], k)
                for i in live:
                    columns[later][i] = columns[later][i] - ratio[i] * entry
            for i in live:
                if i > first or k < 7:
                    blocks[i] = blocks[i] - ratio[i] * row
    return blocks


def dot(a, b, contract=((1,), (0,)), precision=highest):
    return lax.dot_general(a, b, (contract, ((), ())), precision=precision, preferred_element_type=f32)


def left_kernel(momentum_ref, gradient_ref, basis_ref, buffer_ref, copies_ref):
    buffer = momentum_ref[...] + gradient_ref[...].astype(f32)
    buffer_ref[...] = buffer
    part = dot(buffer, basis_ref[...], ((1,), (1,)))
    half = part.shape[0] // 2
    packed = jnp.concatenate([part[:half], part[half:]], axis=1)
    copies_ref[...] = jnp.broadcast_to(packed[None], copies_ref.shape)


def product_kernel(parts_ref, buffer_ref, left_ref, products_ref):
    rank = left_ref.shape[1]
    packed = jnp.sum(parts_ref[...], axis=0)
    left = jnp.concatenate([packed[:, :rank], packed[:, rank:]], axis=0)
    left_ref[...] = left
    turned = left.T
    slabs = buffer_ref.shape[1] // 128
    for slab in range(slabs):
        products_ref[:, slab, :] = dot(turned, buffer_ref[:, 128 * slab:128 * slab + 128])
    gram = dot(turned, left)
    products_ref[:, slabs, :] = jnp.concatenate([gram, jnp.zeros((rank, 128 - rank), f32)], axis=1)


def factor_kernel(whole_ref, left_ref, right_ref, ortho_ref, copies_ref):
    rank = left_ref.shape[1]
    slabs = right_ref.shape[1] // 128
    row = lax.broadcasted_iota(jnp.int32, (rank, 2 * rank), 0)
    column = lax.broadcasted_iota(jnp.int32, (rank, 2 * rank), 1)
    start = jnp.where(column < rank, whole_ref[:, slabs, :], jnp.where(column == row + rank, 1.0, 0.0))
    blocks = eliminate([start[8 * i:8 * i + 8] for i in range(rank // 8)], rank, 2 * rank)
    done = jnp.concatenate(blocks, axis=0)
    pivots = jnp.sum(jnp.where(row == column, done, 0.0), axis=1, keepdims=True)
    inverse = (done / jnp.sqrt(pivots))[:, rank:]
    total = jnp.zeros((rank, 128), f32)
    for slab in range(slabs):
        right = dot(inverse, whole_ref[:, slab, :])
        right_ref[:, 128 * slab:128 * slab + 128] = right
        total = total + right * right
    squares = dot(jnp.ones((8, 128), f32), total, ((1,), (1,)))
    squares = jnp.concatenate([squares, jnp.zeros((8, 128 - rank), f32)], axis=1)
    copies_ref[...] = jnp.broadcast_to(squares[None], copies_ref.shape)
    ortho_ref[...] = dot(left_ref[...], inverse, ((1,), (1,)))


def update_kernel(factor, squares_ref, right_ref, ortho_ref, buffer_ref, weight_ref,
                  new_weight_ref, new_momentum_ref, new_basis_ref):
    rows, rank = ortho_ref.shape
    norms = jnp.sqrt(jnp.sum(squares_ref[...], axis=0))[:1, :rank]
    scale = 1.0 / (norms + tiny_eps)
    row = lax.broadcasted_iota(jnp.int32, (rank, rank), 0)
    column = lax.broadcasted_iota(jnp.int32, (rank, rank), 1)
    turned = jnp.sum(jnp.where(row == column, scale, 0.0), axis=1, keepdims=True)
    right = right_ref[...]
    ortho = ortho_ref[...]
    both = jnp.concatenate([(1.0 - decay_rate) * ortho, factor * (ortho * scale)], axis=0)
    both_high = both.astype(jnp.bfloat16)
    both_low = (both - both_high.astype(f32)).astype(jnp.bfloat16)
    right_high = right.astype(jnp.bfloat16)
    right_low = (right - right_high.astype(f32)).astype(jnp.bfloat16)
    update = dot(
        jnp.concatenate([both_high, both_low, both_high], axis=1),
        jnp.concatenate([right_high, right_high, right_low], axis=0),
        precision=lax.Precision.DEFAULT,
    )
    new_momentum_ref[...] = buffer_ref[...] - update[:rows]
    new_weight_ref[...] = weight_ref[...] - update[rows:]
    new_basis_ref[...] = right * turned


def call(kernel, name, args, shapes):
    in_vmem = pl.BlockSpec(memory_space=pltpu.VMEM)
    return pl.pallas_call(
        kernel,
        out_shape=[jax.ShapeDtypeStruct(shape, f32) for shape in shapes],
        in_specs=[in_vmem] * len(args),
        out_specs=[in_vmem] * len(shapes),
        name=name,
    )(*args)


def per_device(weight, momentum, gradient, right_basis):
    rank = right_basis.shape[1]
    rows, cols = weight.shape
    fsdp, tensor = lax.axis_size("fsdp"), lax.axis_size("tensor")
    buffer, parts = call(
        left_kernel, "left", (momentum, gradient, right_basis.T),
        [(rows, cols), (tensor, rows // 2, 2 * rank)])
    parts = exchange(parts, "tensor")
    left, products = call(product_kernel, "products", (parts, buffer), [(rows, rank), (rank, 8, 128)])
    mine = jnp.sum(exchange(products, "fsdp"), axis=0)
    whole = exchange(copies(mine, "fsdp"), "fsdp")
    right, ortho, squares = call(
        factor_kernel, "factor", (whole, left),
        [(rank, cols), (rows, rank), (tensor, 8, 128)])
    squares = exchange(squares, "tensor")
    factor = step_size * math.sqrt(rows * fsdp * cols * tensor / rank)
    new_weight, new_momentum, new_basis = call(
        functools.partial(update_kernel, factor), "update", (squares, right, ortho, buffer, weight),
        [(rows, cols), (rows, cols), (rank, cols)])
    return (new_weight, new_momentum, new_basis.T)


def solution(mesh):
    placed = (P("fsdp", "tensor"), P("fsdp", "tensor"), P("fsdp", "tensor"), P("tensor", None))
    return jax.shard_map(
        per_device,
        mesh=mesh,
        in_specs=placed,
        out_specs=(P("fsdp", "tensor"), P("fsdp", "tensor"), P("tensor", None)),
        check_vma=False,
    )
```

```python
import functools
import math

import jax
import jax.numpy as jnp
from jax import lax
from jax.experimental import pallas as pl
from jax.experimental.pallas import tpu as pltpu
from jax.sharding import PartitionSpec as P

decay_rate = 0.95
step_size = 0.3
tiny_eps = 1e-08
highest = lax.Precision.HIGHEST
f32 = jnp.float32


def exchange(blocks, axis):
    return lax.all_to_all(blocks, axis, 0, 0)


def copies(block, axis):
    return jnp.broadcast_to(block[None], (lax.axis_size(axis),) + block.shape)


def eliminate(blocks, size, width):
    sublane = lax.broadcasted_iota(jnp.int32, (8, width), 0)

    def spread_row(block, row):
        return jnp.broadcast_to(block[row:row + 1, :], (8, width))

    def spread_column(block, column):
        return jnp.broadcast_to(block[:, column:column + 1], (8, width))

    count = size // 8
    for first in range(count):
        live = range(first, count)
        columns = [{i: spread_column(blocks[i], 8 * first + k) for i in live} for k in range(8)]
        for k in range(8):
            inverse = 1.0 / spread_row(columns[k][first], k)
            row = spread_row(blocks[first], k)
            ratio = {i: columns[k][i] * inverse for i in live}
            ratio[first] = jnp.where(sublane > k, ratio[first], 0.0)
            for later in range(k + 1, 8):
                entry = spread_row(columns[later][first], k)
                for i in live:
                    columns[later][i] = columns[later][i] - ratio[i] * entry
            for i in live:
                if i > first or k < 7:
                    blocks[i] = blocks[i] - ratio[i] * row
    return blocks


def dot(a, b, contract=((1,), (0,)), precision=highest):
    return lax.dot_general(a, b, (contract, ((), ())), precision=precision, preferred_element_type=f32)


def terms(x, count):
    parts = []
    for _ in range(count):
        parts.append(x.astype(jnp.bfloat16))
        x = x - parts[-1].astype(f32)
    return parts


def stacked(a, b, depth):
    a, b = terms(a, depth), terms(b, depth)
    pairs = [(i, j) for i in range(depth) for j in range(depth) if i + j < depth]
    return dot(
        jnp.concatenate([a[i] for i, _ in pairs], axis=1),
        jnp.concatenate([b[j] for _, j in pairs], axis=0),
        precision=lax.Precision.DEFAULT,
    )


def left_kernel(buffer_ref, basis_ref, copies_ref):
    part = dot(buffer_ref[...], basis_ref[...], ((1,), (1,)))
    half = part.shape[0] // 2
    packed = jnp.concatenate([part[:half], part[half:]], axis=1)
    copies_ref[...] = jnp.broadcast_to(packed[None], copies_ref.shape)


def product_kernel(parts_ref, buffer_ref, left_ref, products_ref):
    rank = left_ref.shape[1]
    packed = jnp.sum(parts_ref[...], axis=0)
    left = jnp.concatenate([packed[:, :rank], packed[:, rank:]], axis=0)
    left_ref[...] = left
    padded = jnp.concatenate([left, jnp.zeros((left.shape[0], 128 - rank), f32)], axis=1)
    products = stacked(left.T, jnp.concatenate([buffer_ref[...], padded], axis=1), 3)
    slabs = [products[:, i:i + 128] for i in range(0, products.shape[1], 128)]
    products_ref[...] = jnp.swapaxes(jnp.stack(slabs, axis=0), 0, 1)


def factor_kernel(whole_ref, left_ref, right_ref, ortho_ref, copies_ref):
    rank = left_ref.shape[1]
    slabs = right_ref.shape[1] // 128
    row = lax.broadcasted_iota(jnp.int32, (rank, 2 * rank), 0)
    column = lax.broadcasted_iota(jnp.int32, (rank, 2 * rank), 1)
    start = jnp.where(column < rank, whole_ref[:, slabs, :], jnp.where(column == row + rank, 1.0, 0.0))
    blocks = eliminate([start[8 * i:8 * i + 8] for i in range(rank // 8)], rank, 2 * rank)
    done = jnp.concatenate(blocks, axis=0)
    pivots = jnp.sum(jnp.where(row == column, done, 0.0), axis=1, keepdims=True)
    inverse = (done / jnp.sqrt(pivots))[:, rank:]
    right = stacked(inverse, jnp.concatenate([whole_ref[:, i, :] for i in range(slabs)], axis=1), 3)
    right_ref[...] = right
    total = sum(right[:, 128 * i:128 * i + 128] * right[:, 128 * i:128 * i + 128] for i in range(slabs))
    squares = dot(jnp.ones((8, 128), f32), total, ((1,), (1,)))
    squares = jnp.concatenate([squares, jnp.zeros((8, 128 - rank), f32)], axis=1)
    copies_ref[...] = jnp.broadcast_to(squares[None], copies_ref.shape)
    ortho_ref[...] = dot(left_ref[...], inverse, ((1,), (1,)))


def update_kernel(factor, squares_ref, right_ref, ortho_ref, buffer_ref, weight_ref,
                  new_weight_ref, new_momentum_ref, new_basis_ref):
    rows, rank = ortho_ref.shape
    norms = jnp.sqrt(jnp.sum(squares_ref[...], axis=0))[:1, :rank]
    scale = 1.0 / (norms + tiny_eps)
    row = lax.broadcasted_iota(jnp.int32, (rank, rank), 0)
    column = lax.broadcasted_iota(jnp.int32, (rank, rank), 1)
    turned = jnp.sum(jnp.where(row == column, scale, 0.0), axis=1, keepdims=True)
    right = right_ref[...]
    ortho = ortho_ref[...]
    both = jnp.concatenate([(1.0 - decay_rate) * ortho, factor * (ortho * scale)], axis=0)
    update = stacked(both, right, 2)
    new_momentum_ref[...] = buffer_ref[...] - update[:rows]
    new_weight_ref[...] = weight_ref[...] - update[rows:]
    new_basis_ref[...] = right * turned


def call(kernel, name, args, shapes):
    in_vmem = pl.BlockSpec(memory_space=pltpu.VMEM)
    return pl.pallas_call(
        kernel,
        out_shape=[jax.ShapeDtypeStruct(shape, f32) for shape in shapes],
        in_specs=[in_vmem] * len(args),
        out_specs=[in_vmem] * len(shapes),
        compiler_params=pltpu.CompilerParams(vmem_limit_bytes=16 * 2**20),
        name=name,
    )(*args)


def per_device(weight, momentum, gradient, right_basis):
    rank = right_basis.shape[1]
    rows, cols = weight.shape
    fsdp, tensor = lax.axis_size("fsdp"), lax.axis_size("tensor")
    buffer = momentum + gradient.astype(f32)
    (parts,) = call(left_kernel, "left", (buffer, right_basis.T), [(tensor, rows // 2, 2 * rank)])
    parts = exchange(parts, "tensor")
    left, products = call(product_kernel, "products", (parts, buffer), [(rows, rank), (rank, 8, 128)])
    mine = jnp.sum(exchange(products, "fsdp"), axis=0)
    whole = exchange(copies(mine, "fsdp"), "fsdp")
    right, ortho, squares = call(
        factor_kernel, "factor", (whole, left),
        [(rank, cols), (rows, rank), (tensor, 8, 128)])
    squares = exchange(squares, "tensor")
    factor = step_size * math.sqrt(rows * fsdp * cols * tensor / rank)
    new_weight, new_momentum, new_basis = call(
        functools.partial(update_kernel, factor), "update", (squares, right, ortho, buffer, weight),
        [(rows, cols), (rows, cols), (rank, cols)])
    return (new_weight, new_momentum, new_basis.T)


def solution(mesh):
    placed = (P("fsdp", "tensor"), P("fsdp", "tensor"), P("fsdp", "tensor"), P("tensor", None))
    return jax.shard_map(
        per_device,
        mesh=mesh,
        in_specs=placed,
        out_specs=(P("fsdp", "tensor"), P("fsdp", "tensor"), P("tensor", None)),
        check_vma=False,
    )
```

```python
import functools
import math

import jax
import jax.numpy as jnp
from jax import lax
from jax.experimental import pallas as pl
from jax.experimental.pallas import tpu as pltpu
from jax.sharding import PartitionSpec as P

decay_rate = 0.95
step_size = 0.3
tiny_eps = 1e-08
highest = lax.Precision.HIGHEST
f32 = jnp.float32


def exchange(blocks, axis, groups=None):
    return lax.all_to_all(blocks, axis, 0, 0, axis_index_groups=groups)


def copies(block, count):
    return jnp.broadcast_to(block[None], (count,) + block.shape)


def sum_over_fsdp(blocks):
    side = math.isqrt(lax.axis_size("fsdp"))
    lines = [[side * i + j for j in range(side)] for i in range(side)]
    across = [list(line) for line in zip(*lines)]
    parts = blocks.reshape(side, -1, blocks.shape[-1])
    mine = jnp.sum(exchange(parts, "fsdp", lines), axis=0)
    mine = jnp.sum(exchange(copies(mine, side), "fsdp", across), axis=0)
    return exchange(copies(mine, side), "fsdp", lines).reshape(blocks.shape)


def eliminate(blocks, size, width):
    sublane = lax.broadcasted_iota(jnp.int32, (8, width), 0)

    def spread_row(block, row):
        return jnp.broadcast_to(block[row:row + 1, :], (8, width))

    def spread_column(block, column):
        return jnp.broadcast_to(block[:, column:column + 1], (8, width))

    count = size // 8
    for first in range(count):
        live = range(first, count)
        columns = [{i: spread_column(blocks[i], 8 * first + k) for i in live} for k in range(8)]
        for k in range(8):
            inverse = 1.0 / spread_row(columns[k][first], k)
            row = spread_row(blocks[first], k)
            ratio = {i: columns[k][i] * inverse for i in live}
            ratio[first] = jnp.where(sublane > k, ratio[first], 0.0)
            for later in range(k + 1, 8):
                entry = spread_row(columns[later][first], k)
                for i in live:
                    columns[later][i] = columns[later][i] - ratio[i] * entry
            for i in live:
                if i > first or k < 7:
                    blocks[i] = blocks[i] - ratio[i] * row
    return blocks


def dot(a, b, contract=((1,), (0,)), precision=highest):
    return lax.dot_general(a, b, (contract, ((), ())), precision=precision, preferred_element_type=f32)


def terms(x, count):
    parts = []
    for _ in range(count):
        parts.append(x.astype(jnp.bfloat16))
        x = x - parts[-1].astype(f32)
    return parts


def stacked(a, b, depth):
    a, b = terms(a, depth), terms(b, depth)
    pairs = [(i, j) for i in range(depth) for j in range(depth) if i + j < depth]
    return dot(
        jnp.concatenate([a[i] for i, _ in pairs], axis=1),
        jnp.concatenate([b[j] for _, j in pairs], axis=0),
        precision=lax.Precision.DEFAULT,
    )


def left_kernel(buffer_ref, basis_ref, copies_ref):
    part = dot(buffer_ref[...], basis_ref[...], ((1,), (1,)))
    half = part.shape[0] // 2
    packed = jnp.concatenate([part[:half], part[half:]], axis=1)
    copies_ref[...] = jnp.broadcast_to(packed[None], copies_ref.shape)


def product_kernel(parts_ref, buffer_ref, left_ref, products_ref):
    rank = left_ref.shape[1]
    packed = jnp.sum(parts_ref[...], axis=0)
    left = jnp.concatenate([packed[:, :rank], packed[:, rank:]], axis=0)
    left_ref[...] = left
    padded = jnp.concatenate([left, jnp.zeros((left.shape[0], 128 - rank), f32)], axis=1)
    products = stacked(left.T, jnp.concatenate([buffer_ref[...], padded], axis=1), 3)
    slabs = [products[:, i:i + 128] for i in range(0, products.shape[1], 128)]
    products_ref[...] = jnp.swapaxes(jnp.stack(slabs, axis=0), 0, 1)


def factor_kernel(whole_ref, left_ref, right_ref, ortho_ref, copies_ref):
    rank = left_ref.shape[1]
    slabs = right_ref.shape[1] // 128
    row = lax.broadcasted_iota(jnp.int32, (rank, 2 * rank), 0)
    column = lax.broadcasted_iota(jnp.int32, (rank, 2 * rank), 1)
    start = jnp.where(column < rank, whole_ref[:, slabs, :], jnp.where(column == row + rank, 1.0, 0.0))
    blocks = eliminate([start[8 * i:8 * i + 8] for i in range(rank // 8)], rank, 2 * rank)
    done = jnp.concatenate(blocks, axis=0)
    pivots = jnp.sum(jnp.where(row == column, done, 0.0), axis=1, keepdims=True)
    inverse = (done / jnp.sqrt(pivots))[:, rank:]
    right = stacked(inverse, jnp.concatenate([whole_ref[:, i, :] for i in range(slabs)], axis=1), 3)
    right_ref[...] = right
    total = sum(right[:, 128 * i:128 * i + 128] * right[:, 128 * i:128 * i + 128] for i in range(slabs))
    squares = dot(jnp.ones((8, 128), f32), total, ((1,), (1,)))
    squares = jnp.concatenate([squares, jnp.zeros((8, 128 - rank), f32)], axis=1)
    copies_ref[...] = jnp.broadcast_to(squares[None], copies_ref.shape)
    ortho_ref[...] = dot(left_ref[...], inverse, ((1,), (1,)))


def update_kernel(factor, squares_ref, right_ref, ortho_ref, buffer_ref, weight_ref,
                  new_weight_ref, new_momentum_ref, new_basis_ref):
    rows, rank = ortho_ref.shape
    norms = jnp.sqrt(jnp.sum(squares_ref[...], axis=0))[:1, :rank]
    scale = 1.0 / (norms + tiny_eps)
    row = lax.broadcasted_iota(jnp.int32, (rank, rank), 0)
    column = lax.broadcasted_iota(jnp.int32, (rank, rank), 1)
    turned = jnp.sum(jnp.where(row == column, scale, 0.0), axis=1, keepdims=True)
    right = right_ref[...]
    ortho = ortho_ref[...]
    both = jnp.concatenate([(1.0 - decay_rate) * ortho, factor * (ortho * scale)], axis=0)
    update = stacked(both, right, 2)
    new_momentum_ref[...] = buffer_ref[...] - update[:rows]
    new_weight_ref[...] = weight_ref[...] - update[rows:]
    new_basis_ref[...] = right * turned


def call(kernel, name, args, shapes):
    in_vmem = pl.BlockSpec(memory_space=pltpu.VMEM)
    return pl.pallas_call(
        kernel,
        out_shape=[jax.ShapeDtypeStruct(shape, f32) for shape in shapes],
        in_specs=[in_vmem] * len(args),
        out_specs=[in_vmem] * len(shapes),
        compiler_params=pltpu.CompilerParams(vmem_limit_bytes=16 * 2**20),
        name=name,
    )(*args)


def per_device(weight, momentum, gradient, right_basis):
    rank = right_basis.shape[1]
    rows, cols = weight.shape
    fsdp, tensor = lax.axis_size("fsdp"), lax.axis_size("tensor")
    buffer = momentum + gradient.astype(f32)
    (parts,) = call(left_kernel, "left", (buffer, right_basis.T), [(tensor, rows // 2, 2 * rank)])
    parts = exchange(parts, "tensor")
    left, products = call(product_kernel, "products", (parts, buffer), [(rows, rank), (rank, 8, 128)])
    whole = sum_over_fsdp(products)
    right, ortho, squares = call(
        factor_kernel, "factor", (whole, left),
        [(rank, cols), (rows, rank), (tensor, 8, 128)])
    squares = exchange(squares, "tensor")
    factor = step_size * math.sqrt(rows * fsdp * cols * tensor / rank)
    new_weight, new_momentum, new_basis = call(
        functools.partial(update_kernel, factor), "update", (squares, right, ortho, buffer, weight),
        [(rows, cols), (rows, cols), (rank, cols)])
    return (new_weight, new_momentum, new_basis.T)


def solution(mesh):
    placed = (P("fsdp", "tensor"), P("fsdp", "tensor"), P("fsdp", "tensor"), P("tensor", None))
    return jax.shard_map(
        per_device,
        mesh=mesh,
        in_specs=placed,
        out_specs=(P("fsdp", "tensor"), P("fsdp", "tensor"), P("tensor", None)),
        check_vma=False,
    )
```

```python
import functools
import math

import jax
import jax.numpy as jnp
from jax import lax
from jax.experimental import pallas as pl
from jax.experimental.pallas import tpu as pltpu
from jax.sharding import PartitionSpec as P

decay_rate = 0.95
step_size = 0.3
tiny_eps = 1e-08
highest = lax.Precision.HIGHEST
f32 = jnp.float32


def exchange(blocks, axis):
    return lax.all_to_all(blocks, axis, 0, 0, axis_index_groups=[order(axis)])


def order(axis):
    count = lax.axis_size(axis)
    if axis == "tensor":
        return list(range(count))[::-1]
    side = math.isqrt(count)
    turned = [(i + 4) % side for i in range(side)]
    return [side * y + x for y in turned for x in turned]


def copies(block, axis):
    return jnp.broadcast_to(block[None], (lax.axis_size(axis),) + block.shape)


def eliminate(blocks, size, width):
    sublane = lax.broadcasted_iota(jnp.int32, (8, width), 0)

    def spread_row(block, row):
        return jnp.broadcast_to(block[row:row + 1, :], (8, width))

    def spread_column(block, column):
        return jnp.broadcast_to(block[:, column:column + 1], (8, width))

    count = size // 8
    for first in range(count):
        live = range(first, count)
        columns = [{i: spread_column(blocks[i], 8 * first + k) for i in live} for k in range(8)]
        for k in range(8):
            inverse = 1.0 / spread_row(columns[k][first], k)
            row = spread_row(blocks[first], k)
            ratio = {i: columns[k][i] * inverse for i in live}
            ratio[first] = jnp.where(sublane > k, ratio[first], 0.0)
            for later in range(k + 1, 8):
                entry = spread_row(columns[later][first], k)
                for i in live:
                    columns[later][i] = columns[later][i] - ratio[i] * entry
            for i in live:
                if i > first or k < 7:
                    blocks[i] = blocks[i] - ratio[i] * row
    return blocks


def dot(a, b, contract=((1,), (0,)), precision=highest):
    return lax.dot_general(a, b, (contract, ((), ())), precision=precision, preferred_element_type=f32)


def terms(x, count):
    parts = []
    for _ in range(count):
        parts.append(x.astype(jnp.bfloat16))
        x = x - parts[-1].astype(f32)
    return parts


def stacked(a, b, depth):
    a, b = terms(a, depth), terms(b, depth)
    pairs = [(i, j) for i in range(depth) for j in range(depth) if i + j < depth]
    return dot(
        jnp.concatenate([a[i] for i, _ in pairs], axis=1),
        jnp.concatenate([b[j] for _, j in pairs], axis=0),
        precision=lax.Precision.DEFAULT,
    )


def left_kernel(buffer_ref, basis_ref, copies_ref):
    part = dot(buffer_ref[...], basis_ref[...], ((1,), (1,)))
    half = part.shape[0] // 2
    packed = jnp.concatenate([part[:half], part[half:]], axis=1)
    copies_ref[...] = jnp.broadcast_to(packed[None], copies_ref.shape)


def product_kernel(parts_ref, buffer_ref, left_ref, products_ref):
    rank = left_ref.shape[1]
    packed = jnp.sum(parts_ref[...], axis=0)
    left = jnp.concatenate([packed[:, :rank], packed[:, rank:]], axis=0)
    left_ref[...] = left
    padded = jnp.concatenate([left, jnp.zeros((left.shape[0], 128 - rank), f32)], axis=1)
    products = stacked(left.T, jnp.concatenate([buffer_ref[...], padded], axis=1), 3)
    slabs = [products[:, i:i + 128] for i in range(0, products.shape[1], 128)]
    products_ref[...] = jnp.swapaxes(jnp.stack(slabs, axis=0), 0, 1)


def factor_kernel(whole_ref, left_ref, right_ref, ortho_ref, copies_ref):
    rank = left_ref.shape[1]
    slabs = right_ref.shape[1] // 128
    row = lax.broadcasted_iota(jnp.int32, (rank, 2 * rank), 0)
    column = lax.broadcasted_iota(jnp.int32, (rank, 2 * rank), 1)
    start = jnp.where(column < rank, whole_ref[:, slabs, :], jnp.where(column == row + rank, 1.0, 0.0))
    blocks = eliminate([start[8 * i:8 * i + 8] for i in range(rank // 8)], rank, 2 * rank)
    done = jnp.concatenate(blocks, axis=0)
    pivots = jnp.sum(jnp.where(row == column, done, 0.0), axis=1, keepdims=True)
    inverse = (done / jnp.sqrt(pivots))[:, rank:]
    right = stacked(inverse, jnp.concatenate([whole_ref[:, i, :] for i in range(slabs)], axis=1), 3)
    right_ref[...] = right
    total = sum(right[:, 128 * i:128 * i + 128] * right[:, 128 * i:128 * i + 128] for i in range(slabs))
    squares = dot(jnp.ones((8, 128), f32), total, ((1,), (1,)))
    squares = jnp.concatenate([squares, jnp.zeros((8, 128 - rank), f32)], axis=1)
    copies_ref[...] = jnp.broadcast_to(squares[None], copies_ref.shape)
    ortho_ref[...] = dot(left_ref[...], inverse, ((1,), (1,)))


def update_kernel(factor, squares_ref, right_ref, ortho_ref, buffer_ref, weight_ref,
                  new_weight_ref, new_momentum_ref, new_basis_ref):
    rows, rank = ortho_ref.shape
    norms = jnp.sqrt(jnp.sum(squares_ref[...], axis=0))[:1, :rank]
    scale = 1.0 / (norms + tiny_eps)
    row = lax.broadcasted_iota(jnp.int32, (rank, rank), 0)
    column = lax.broadcasted_iota(jnp.int32, (rank, rank), 1)
    turned = jnp.sum(jnp.where(row == column, scale, 0.0), axis=1, keepdims=True)
    right = right_ref[...]
    ortho = ortho_ref[...]
    both = jnp.concatenate([(1.0 - decay_rate) * ortho, factor * (ortho * scale)], axis=0)
    update = stacked(both, right, 2)
    new_momentum_ref[...] = buffer_ref[...] - update[:rows]
    new_weight_ref[...] = weight_ref[...] - update[rows:]
    new_basis_ref[...] = right * turned


def call(kernel, name, args, shapes):
    in_vmem = pl.BlockSpec(memory_space=pltpu.VMEM)
    return pl.pallas_call(
        kernel,
        out_shape=[jax.ShapeDtypeStruct(shape, f32) for shape in shapes],
        in_specs=[in_vmem] * len(args),
        out_specs=[in_vmem] * len(shapes),
        compiler_params=pltpu.CompilerParams(vmem_limit_bytes=16 * 2**20),
        name=name,
    )(*args)


def per_device(weight, momentum, gradient, right_basis):
    rank = right_basis.shape[1]
    rows, cols = weight.shape
    fsdp, tensor = lax.axis_size("fsdp"), lax.axis_size("tensor")
    buffer = momentum + gradient.astype(f32)
    (parts,) = call(left_kernel, "left", (buffer, right_basis.T), [(tensor, rows // 2, 2 * rank)])
    parts = exchange(parts, "tensor")
    left, products = call(product_kernel, "products", (parts, buffer), [(rows, rank), (rank, 8, 128)])
    mine = jnp.sum(exchange(products, "fsdp"), axis=0)
    whole = exchange(copies(mine, "fsdp"), "fsdp")
    right, ortho, squares = call(
        factor_kernel, "factor", (whole, left),
        [(rank, cols), (rows, rank), (tensor, 8, 128)])
    squares = exchange(squares, "tensor")
    factor = step_size * math.sqrt(rows * fsdp * cols * tensor / rank)
    new_weight, new_momentum, new_basis = call(
        functools.partial(update_kernel, factor), "update", (squares, right, ortho, buffer, weight),
        [(rows, cols), (rows, cols), (rank, cols)])
    return (new_weight, new_momentum, new_basis.T)


def solution(mesh):
    placed = (P("fsdp", "tensor"), P("fsdp", "tensor"), P("fsdp", "tensor"), P("tensor", None))
    return jax.shard_map(
        per_device,
        mesh=mesh,
        in_specs=placed,
        out_specs=(P("fsdp", "tensor"), P("fsdp", "tensor"), P("tensor", None)),
        check_vma=False,
    )
```

```python
import functools
import math

import jax
import jax.numpy as jnp
from jax import lax
from jax.experimental import pallas as pl
from jax.experimental.pallas import tpu as pltpu
from jax.sharding import PartitionSpec as P

decay_rate = 0.95
step_size = 0.3
tiny_eps = 1e-08
highest = lax.Precision.HIGHEST
f32 = jnp.float32


def exchange(blocks, axis):
    return lax.all_to_all(blocks, axis, 0, 0, axis_index_groups=[order(axis)])


def order(axis):
    count = lax.axis_size(axis)
    if axis == "tensor":
        return list(range(count))[::-1]
    side = math.isqrt(count)
    turned = [(i + 4) % side for i in range(side)]
    return [side * y + x for y in turned for x in turned]


def copies(block, axis):
    return jnp.broadcast_to(block[None], (lax.axis_size(axis),) + block.shape)


def eliminate(blocks, size, width):
    sublane = lax.broadcasted_iota(jnp.int32, (8, width), 0)

    def spread_row(block, row):
        return jnp.broadcast_to(block[row:row + 1, :], (8, width))

    def spread_column(block, column):
        return jnp.broadcast_to(block[:, column:column + 1], (8, width))

    count = size // 8
    for first in range(count):
        live = range(first, count)
        columns = [{i: spread_column(blocks[i], 8 * first + k) for i in live} for k in range(8)]
        for k in range(8):
            inverse = 1.0 / spread_row(columns[k][first], k)
            row = spread_row(blocks[first], k)
            ratio = {i: columns[k][i] * inverse for i in live}
            below = jnp.where(sublane > k, ratio[first], 0.0)
            for later in range(k + 1, 8):
                entry = spread_row(columns[later][first], k)
                for i in live:
                    columns[later][i] = columns[later][i] - ratio[i] * entry
            if k < 7:
                blocks[first] = blocks[first] - below * row
            for i in range(first + 1, count):
                blocks[i] = blocks[i] - ratio[i] * row
    return blocks


def dot(a, b, contract=((1,), (0,)), precision=highest):
    return lax.dot_general(a, b, (contract, ((), ())), precision=precision, preferred_element_type=f32)


def terms(x, count):
    parts = []
    for _ in range(count):
        parts.append(x.astype(jnp.bfloat16))
        x = x - parts[-1].astype(f32)
    return parts


def stacked(a, b, depth):
    a, b = terms(a, depth), terms(b, depth)
    pairs = [(i, j) for i in range(depth) for j in range(depth) if i + j < depth]
    return dot(
        jnp.concatenate([a[i] for i, _ in pairs], axis=1),
        jnp.concatenate([b[j] for _, j in pairs], axis=0),
        precision=lax.Precision.DEFAULT,
    )


def left_kernel(buffer_ref, basis_ref, copies_ref):
    part = dot(buffer_ref[...], basis_ref[...], ((1,), (1,)))
    half = part.shape[0] // 2
    packed = jnp.concatenate([part[:half], part[half:]], axis=1)
    copies_ref[...] = jnp.broadcast_to(packed[None], copies_ref.shape)


def product_kernel(parts_ref, buffer_ref, left_ref, products_ref):
    rank = left_ref.shape[1]
    packed = jnp.sum(parts_ref[...], axis=0)
    left = jnp.concatenate([packed[:, :rank], packed[:, rank:]], axis=0)
    left_ref[...] = left
    padded = jnp.concatenate([left, jnp.zeros((left.shape[0], 128 - rank), f32)], axis=1)
    products = stacked(left.T, jnp.concatenate([buffer_ref[...], padded], axis=1), 3)
    slabs = [products[:, i:i + 128] for i in range(0, products.shape[1], 128)]
    products_ref[...] = jnp.swapaxes(jnp.stack(slabs, axis=0), 0, 1)


def factor_kernel(whole_ref, left_ref, right_ref, ortho_ref, copies_ref):
    rank = left_ref.shape[1]
    slabs = right_ref.shape[1] // 128
    row = lax.broadcasted_iota(jnp.int32, (rank, 2 * rank), 0)
    column = lax.broadcasted_iota(jnp.int32, (rank, 2 * rank), 1)
    start = jnp.where(column < rank, whole_ref[:, slabs, :], jnp.where(column == row + rank, 1.0, 0.0))
    blocks = eliminate([start[8 * i:8 * i + 8] for i in range(rank // 8)], rank, 2 * rank)
    done = jnp.concatenate(blocks, axis=0)
    pivots = jnp.sum(jnp.where(row == column, done, 0.0), axis=1, keepdims=True)
    inverse = (done / jnp.sqrt(pivots))[:, rank:]
    right = stacked(inverse, jnp.concatenate([whole_ref[:, i, :] for i in range(slabs)], axis=1), 3)
    right_ref[...] = right
    total = sum(right[:, 128 * i:128 * i + 128] * right[:, 128 * i:128 * i + 128] for i in range(slabs))
    squares = dot(jnp.ones((8, 128), f32), total, ((1,), (1,)))[:1]
    squares = jnp.concatenate([squares, jnp.zeros((1, 128 - rank), f32)], axis=1)
    copies_ref[...] = jnp.broadcast_to(squares[None], copies_ref.shape)
    ortho_ref[...] = dot(left_ref[...], inverse, ((1,), (1,)))


def update_kernel(factor, squares_ref, right_ref, ortho_ref, buffer_ref, weight_ref,
                  new_weight_ref, new_momentum_ref, new_basis_ref):
    rows, rank = ortho_ref.shape
    norms = jnp.sqrt(jnp.sum(squares_ref[...], axis=0))[:, :rank]
    scale = 1.0 / (norms + tiny_eps)
    row = lax.broadcasted_iota(jnp.int32, (rank, rank), 0)
    column = lax.broadcasted_iota(jnp.int32, (rank, rank), 1)
    turned = jnp.sum(jnp.where(row == column, scale, 0.0), axis=1, keepdims=True)
    right = right_ref[...]
    ortho = ortho_ref[...]
    both = jnp.concatenate([(1.0 - decay_rate) * ortho, factor * (ortho * scale)], axis=0)
    update = stacked(both, right, 2)
    new_momentum_ref[...] = buffer_ref[...] - update[:rows]
    new_weight_ref[...] = weight_ref[...] - update[rows:]
    new_basis_ref[...] = right * turned


def call(kernel, name, args, shapes):
    in_vmem = pl.BlockSpec(memory_space=pltpu.VMEM)
    return pl.pallas_call(
        kernel,
        out_shape=[jax.ShapeDtypeStruct(shape, f32) for shape in shapes],
        in_specs=[in_vmem] * len(args),
        out_specs=[in_vmem] * len(shapes),
        compiler_params=pltpu.CompilerParams(vmem_limit_bytes=16 * 2**20),
        name=name,
    )(*args)


def per_device(weight, momentum, gradient, right_basis):
    rank = right_basis.shape[1]
    rows, cols = weight.shape
    fsdp, tensor = lax.axis_size("fsdp"), lax.axis_size("tensor")
    buffer = momentum + gradient.astype(f32)
    (parts,) = call(left_kernel, "left", (buffer, right_basis.T), [(tensor, rows // 2, 2 * rank)])
    parts = exchange(parts, "tensor")
    left, products = call(product_kernel, "products", (parts, buffer), [(rows, rank), (rank, 8, 128)])
    mine = jnp.sum(exchange(products, "fsdp"), axis=0)
    whole = exchange(copies(mine, "fsdp"), "fsdp")
    right, ortho, squares = call(
        factor_kernel, "factor", (whole, left),
        [(rank, cols), (rows, rank), (tensor, 1, 128)])
    squares = exchange(squares, "tensor")
    factor = step_size * math.sqrt(rows * fsdp * cols * tensor / rank)
    new_weight, new_momentum, new_basis = call(
        functools.partial(update_kernel, factor), "update", (squares, right, ortho, buffer, weight),
        [(rows, cols), (rows, cols), (rank, cols)])
    return (new_weight, new_momentum, new_basis.T)


def solution(mesh):
    placed = (P("fsdp", "tensor"), P("fsdp", "tensor"), P("fsdp", "tensor"), P("tensor", None))
    return jax.shard_map(
        per_device,
        mesh=mesh,
        in_specs=placed,
        out_specs=(P("fsdp", "tensor"), P("fsdp", "tensor"), P("tensor", None)),
        check_vma=False,
    )
```

```python
import functools
import math

import jax
import jax.numpy as jnp
from jax import lax
from jax.experimental import pallas as pl
from jax.experimental.pallas import tpu as pltpu
from jax.sharding import PartitionSpec as P

decay_rate = 0.95
step_size = 0.3
tiny_eps = 1e-08
highest = lax.Precision.HIGHEST
f32 = jnp.float32


def exchange(blocks, axis):
    return lax.all_to_all(blocks, axis, 0, 0, axis_index_groups=[order(axis)])


def order(axis):
    count = lax.axis_size(axis)
    if axis == "tensor":
        planes = count // 2
        others = sorted(range(planes - 1), key=lambda z: (min(z, planes - z), -z))
        return [2 * z + core for z in [planes - 1] + others for core in (1, 0)]
    side = math.isqrt(count)
    turned = [(i + 4) % side for i in range(side)]
    return [side * y + x for y in turned for x in turned]


def copies(block, axis):
    return jnp.broadcast_to(block[None], (lax.axis_size(axis),) + block.shape)


def eliminate(blocks, size, width):
    sublane = lax.broadcasted_iota(jnp.int32, (8, width), 0)

    def spread_row(block, row):
        return jnp.broadcast_to(block[row:row + 1, :], (8, width))

    def spread_column(block, column):
        return jnp.broadcast_to(block[:, column:column + 1], (8, width))

    count = size // 8
    for first in range(count):
        live = range(first, count)
        columns = [{i: spread_column(blocks[i], 8 * first + k) for i in live} for k in range(8)]
        for k in range(8):
            inverse = 1.0 / spread_row(columns[k][first], k)
            row = spread_row(blocks[first], k)
            ratio = {i: columns[k][i] * inverse for i in live}
            below = jnp.where(sublane > k, ratio[first], 0.0)
            for later in range(k + 1, 8):
                entry = spread_row(columns[later][first], k)
                for i in live:
                    columns[later][i] = columns[later][i] - ratio[i] * entry
            if k < 7:
                blocks[first] = blocks[first] - below * row
            for i in range(first + 1, count):
                blocks[i] = blocks[i] - ratio[i] * row
    return blocks


def dot(a, b, contract=((1,), (0,)), precision=highest):
    return lax.dot_general(a, b, (contract, ((), ())), precision=precision, preferred_element_type=f32)


def terms(x, count):
    parts = []
    for _ in range(count):
        parts.append(x.astype(jnp.bfloat16))
        x = x - parts[-1].astype(f32)
    return parts


def stacked(a, b, depth):
    a, b = terms(a, depth), terms(b, depth)
    pairs = [(i, j) for i in range(depth) for j in range(depth) if i + j < depth]
    return dot(
        jnp.concatenate([a[i] for i, _ in pairs], axis=1),
        jnp.concatenate([b[j] for _, j in pairs], axis=0),
        precision=lax.Precision.DEFAULT,
    )


def left_kernel(buffer_ref, basis_ref, copies_ref):
    part = dot(buffer_ref[...], basis_ref[...], ((1,), (1,)))
    half = part.shape[0] // 2
    packed = jnp.concatenate([part[:half], part[half:]], axis=1)
    copies_ref[...] = jnp.broadcast_to(packed[None], copies_ref.shape)


def product_kernel(parts_ref, buffer_ref, left_ref, products_ref):
    rank = left_ref.shape[1]
    packed = jnp.sum(parts_ref[...], axis=0)
    left = jnp.concatenate([packed[:, :rank], packed[:, rank:]], axis=0)
    left_ref[...] = left
    padded = jnp.concatenate([left, jnp.zeros((left.shape[0], 128 - rank), f32)], axis=1)
    products = stacked(left.T, jnp.concatenate([buffer_ref[...], padded], axis=1), 3)
    slabs = [products[:, i:i + 128] for i in range(0, products.shape[1], 128)]
    products_ref[...] = jnp.swapaxes(jnp.stack(slabs, axis=0), 0, 1)


def factor_kernel(whole_ref, left_ref, right_ref, ortho_ref, copies_ref):
    rank = left_ref.shape[1]
    slabs = right_ref.shape[1] // 128
    row = lax.broadcasted_iota(jnp.int32, (rank, 2 * rank), 0)
    column = lax.broadcasted_iota(jnp.int32, (rank, 2 * rank), 1)
    start = jnp.where(column < rank, whole_ref[:, slabs, :], jnp.where(column == row + rank, 1.0, 0.0))
    blocks = eliminate([start[8 * i:8 * i + 8] for i in range(rank // 8)], rank, 2 * rank)
    done = jnp.concatenate(blocks, axis=0)
    pivots = jnp.sum(jnp.where(row == column, done, 0.0), axis=1, keepdims=True)
    inverse = (done / jnp.sqrt(pivots))[:, rank:]
    right = stacked(inverse, jnp.concatenate([whole_ref[:, i, :] for i in range(slabs)], axis=1), 3)
    right_ref[...] = right
    total = sum(right[:, 128 * i:128 * i + 128] * right[:, 128 * i:128 * i + 128] for i in range(slabs))
    squares = dot(jnp.ones((8, 128), f32), total, ((1,), (1,)))[:1]
    squares = jnp.concatenate([squares, jnp.zeros((1, 128 - rank), f32)], axis=1)
    copies_ref[...] = jnp.broadcast_to(squares[None], copies_ref.shape)
    ortho_ref[...] = dot(left_ref[...], inverse, ((1,), (1,)))


def update_kernel(factor, squares_ref, right_ref, ortho_ref, buffer_ref, weight_ref,
                  new_weight_ref, new_momentum_ref, new_basis_ref):
    rows, rank = ortho_ref.shape
    norms = jnp.sqrt(jnp.sum(squares_ref[...], axis=0))[:, :rank]
    scale = 1.0 / (norms + tiny_eps)
    row = lax.broadcasted_iota(jnp.int32, (rank, rank), 0)
    column = lax.broadcasted_iota(jnp.int32, (rank, rank), 1)
    turned = jnp.sum(jnp.where(row == column, scale, 0.0), axis=1, keepdims=True)
    right = right_ref[...]
    ortho = ortho_ref[...]
    both = jnp.concatenate([(1.0 - decay_rate) * ortho, factor * (ortho * scale)], axis=0)
    update = stacked(both, right, 2)
    new_momentum_ref[...] = buffer_ref[...] - update[:rows]
    new_weight_ref[...] = weight_ref[...] - update[rows:]
    new_basis_ref[...] = right * turned


def call(kernel, name, args, shapes):
    in_vmem = pl.BlockSpec(memory_space=pltpu.VMEM)
    return pl.pallas_call(
        kernel,
        out_shape=[jax.ShapeDtypeStruct(shape, f32) for shape in shapes],
        in_specs=[in_vmem] * len(args),
        out_specs=[in_vmem] * len(shapes),
        compiler_params=pltpu.CompilerParams(vmem_limit_bytes=16 * 2**20),
        name=name,
    )(*args)


def per_device(weight, momentum, gradient, right_basis):
    rank = right_basis.shape[1]
    rows, cols = weight.shape
    fsdp, tensor = lax.axis_size("fsdp"), lax.axis_size("tensor")
    buffer = momentum + gradient.astype(f32)
    (parts,) = call(left_kernel, "left", (buffer, right_basis.T), [(tensor, rows // 2, 2 * rank)])
    parts = exchange(parts, "tensor")
    left, products = call(product_kernel, "products", (parts, buffer), [(rows, rank), (rank, 8, 128)])
    mine = jnp.sum(exchange(products, "fsdp"), axis=0)
    whole = exchange(copies(mine, "fsdp"), "fsdp")
    right, ortho, squares = call(
        factor_kernel, "factor", (whole, left),
        [(rank, cols), (rows, rank), (tensor, 1, 128)])
    squares = exchange(squares, "tensor")
    factor = step_size * math.sqrt(rows * fsdp * cols * tensor / rank)
    new_weight, new_momentum, new_basis = call(
        functools.partial(update_kernel, factor), "update", (squares, right, ortho, buffer, weight),
        [(rows, cols), (rows, cols), (rank, cols)])
    return (new_weight, new_momentum, new_basis.T)


def solution(mesh):
    placed = (P("fsdp", "tensor"), P("fsdp", "tensor"), P("fsdp", "tensor"), P("tensor", None))
    return jax.shard_map(
        per_device,
        mesh=mesh,
        in_specs=placed,
        out_specs=(P("fsdp", "tensor"), P("fsdp", "tensor"), P("tensor", None)),
        check_vma=False,
    )
```

```python
import functools
import math

import jax
import jax.numpy as jnp
from jax import lax
from jax.experimental import pallas as pl
from jax.experimental.pallas import tpu as pltpu
from jax.sharding import PartitionSpec as P

decay_rate = 0.95
step_size = 0.3
tiny_eps = 1e-08
highest = lax.Precision.HIGHEST
f32 = jnp.float32


def exchange(blocks, axis):
    return lax.all_to_all(blocks, axis, 0, 0, axis_index_groups=[order(axis)])


def order(axis):
    count = lax.axis_size(axis)
    if axis == "tensor":
        planes = count // 2
        others = sorted(range(planes - 1), key=lambda z: (min(z, planes - z), -z))
        return [2 * z + core for z in [planes - 1] + others for core in (1, 0)]
    side = math.isqrt(count)
    turned = [(i + 4) % side for i in range(side)]
    return [side * y + x for y in turned for x in turned]


def copies(block, axis):
    return jnp.broadcast_to(block[None], (lax.axis_size(axis),) + block.shape)


def eliminate(blocks, size, width):
    sublane = lax.broadcasted_iota(jnp.int32, (8, width), 0)

    def spread_row(block, row):
        return jnp.broadcast_to(block[row:row + 1, :], (8, width))

    def spread_column(block, column):
        return jnp.broadcast_to(block[:, column:column + 1], (8, width))

    count = size // 8
    for first in range(count):
        live = range(first, count)
        columns = [{i: spread_column(blocks[i], 8 * first + k) for i in live} for k in range(8)]
        for k in range(8):
            inverse = 1.0 / spread_row(columns[k][first], k)
            row = spread_row(blocks[first], k)
            ratio = {i: columns[k][i] * inverse for i in live}
            below = jnp.where(sublane > k, ratio[first], 0.0)
            for later in range(k + 1, 8):
                entry = spread_row(columns[later][first], k)
                for i in live:
                    columns[later][i] = columns[later][i] - ratio[i] * entry
            if k < 7:
                blocks[first] = blocks[first] - below * row
            for i in range(first + 1, count):
                blocks[i] = blocks[i] - ratio[i] * row
    return blocks


def dot(a, b, contract=((1,), (0,)), precision=highest):
    return lax.dot_general(a, b, (contract, ((), ())), precision=precision, preferred_element_type=f32)


def terms(x, count):
    parts = []
    for _ in range(count):
        parts.append(x.astype(jnp.bfloat16))
        x = x - parts[-1].astype(f32)
    return parts


def stacked(a, b, depth):
    a, b = terms(a, depth), terms(b, depth)
    pairs = [(i, j) for i in range(depth) for j in range(depth) if i + j < depth]
    return dot(
        jnp.concatenate([a[i] for i, _ in pairs], axis=1),
        jnp.concatenate([b[j] for _, j in pairs], axis=0),
        precision=lax.Precision.DEFAULT,
    )


def left_kernel(buffer_ref, basis_ref, copies_ref):
    part = dot(buffer_ref[...], basis_ref[...], ((1,), (1,)))
    half = part.shape[0] // 2
    packed = jnp.concatenate([part[:half], part[half:]], axis=1)
    copies_ref[...] = jnp.broadcast_to(packed[None], copies_ref.shape)


def product_kernel(parts_ref, buffer_ref, left_ref, products_ref):
    rank = left_ref.shape[1]
    packed = jnp.sum(parts_ref[...], axis=0)
    left = jnp.concatenate([packed[:, :rank], packed[:, rank:]], axis=0)
    left_ref[...] = left
    padded = jnp.concatenate([left, jnp.zeros((left.shape[0], 128 - rank), f32)], axis=1)
    products = stacked(left.T, jnp.concatenate([buffer_ref[...], padded], axis=1), 3)
    slabs = [products[:, i:i + 128] for i in range(0, products.shape[1], 128)]
    products_ref[...] = jnp.swapaxes(jnp.stack(slabs, axis=0), 0, 1)


def factor_kernel(whole_ref, left_ref, right_ref, ortho_ref, copies_ref):
    rank = left_ref.shape[1]
    slabs = right_ref.shape[1] // 128
    row = lax.broadcasted_iota(jnp.int32, (rank, 2 * rank), 0)
    column = lax.broadcasted_iota(jnp.int32, (rank, 2 * rank), 1)
    start = jnp.where(column < rank, whole_ref[:, slabs, :], jnp.where(column == row + rank, 1.0, 0.0))
    blocks = eliminate([start[8 * i:8 * i + 8] for i in range(rank // 8)], rank, 2 * rank)
    done = jnp.concatenate(blocks, axis=0)
    pivots = jnp.sum(jnp.where(row == column, done, 0.0), axis=1, keepdims=True)
    inverse = (done / jnp.sqrt(pivots))[:, rank:]
    right = stacked(inverse, jnp.concatenate([whole_ref[:, i, :] for i in range(slabs)], axis=1), 3)
    right_ref[...] = right
    total = sum(right[:, 128 * i:128 * i + 128] * right[:, 128 * i:128 * i + 128] for i in range(slabs))
    squares = dot(jnp.ones((8, 128), f32), total, ((1,), (1,)))[:1]
    squares = jnp.concatenate([squares, jnp.zeros((1, 128 - rank), f32)], axis=1)
    copies_ref[...] = jnp.broadcast_to(squares[None], copies_ref.shape)
    ortho_ref[...] = dot(left_ref[...], inverse, ((1,), (1,)))


def momentum_kernel(right_ref, ortho_ref, buffer_ref, new_momentum_ref):
    new_momentum_ref[...] = buffer_ref[...] - stacked((1.0 - decay_rate) * ortho_ref[...], right_ref[...], 2)


def weight_kernel(factor, squares_ref, right_ref, ortho_ref, weight_ref, new_weight_ref, new_basis_ref):
    rank = ortho_ref.shape[1]
    norms = jnp.sqrt(jnp.sum(squares_ref[...], axis=0))[:, :rank]
    scale = 1.0 / (norms + tiny_eps)
    row = lax.broadcasted_iota(jnp.int32, (rank, rank), 0)
    column = lax.broadcasted_iota(jnp.int32, (rank, rank), 1)
    turned = jnp.sum(jnp.where(row == column, scale, 0.0), axis=1, keepdims=True)
    right = right_ref[...]
    new_weight_ref[...] = weight_ref[...] - stacked(factor * (ortho_ref[...] * scale), right, 2)
    new_basis_ref[...] = right * turned


def call(kernel, name, args, shapes):
    in_vmem = pl.BlockSpec(memory_space=pltpu.VMEM)
    return pl.pallas_call(
        kernel,
        out_shape=[jax.ShapeDtypeStruct(shape, f32) for shape in shapes],
        in_specs=[in_vmem] * len(args),
        out_specs=[in_vmem] * len(shapes),
        compiler_params=pltpu.CompilerParams(vmem_limit_bytes=16 * 2**20),
        name=name,
    )(*args)


def per_device(weight, momentum, gradient, right_basis):
    rank = right_basis.shape[1]
    rows, cols = weight.shape
    fsdp, tensor = lax.axis_size("fsdp"), lax.axis_size("tensor")
    buffer = momentum + gradient.astype(f32)
    (parts,) = call(left_kernel, "left", (buffer, right_basis.T), [(tensor, rows // 2, 2 * rank)])
    parts = exchange(parts, "tensor")
    left, products = call(product_kernel, "products", (parts, buffer), [(rows, rank), (rank, 8, 128)])
    mine = jnp.sum(exchange(products, "fsdp"), axis=0)
    whole = exchange(copies(mine, "fsdp"), "fsdp")
    right, ortho, squares = call(
        factor_kernel, "factor", (whole, left),
        [(rank, cols), (rows, rank), (tensor, 1, 128)])
    squares = exchange(squares, "tensor")
    factor = step_size * math.sqrt(rows * fsdp * cols * tensor / rank)
    (new_momentum,) = call(momentum_kernel, "momentum", (right, ortho, buffer), [(rows, cols)])
    new_weight, new_basis = call(
        functools.partial(weight_kernel, factor), "weight", (squares, right, ortho, weight),
        [(rows, cols), (rank, cols)])
    return (new_weight, new_momentum, new_basis.T)


def solution(mesh):
    placed = (P("fsdp", "tensor"), P("fsdp", "tensor"), P("fsdp", "tensor"), P("tensor", None))
    return jax.shard_map(
        per_device,
        mesh=mesh,
        in_specs=placed,
        out_specs=(P("fsdp", "tensor"), P("fsdp", "tensor"), P("tensor", None)),
        check_vma=False,
    )
```

```python
import functools
import math

import jax
import jax.numpy as jnp
from jax import lax
from jax.experimental import pallas as pl
from jax.experimental.pallas import tpu as pltpu
from jax.sharding import PartitionSpec as P

decay_rate = 0.95
step_size = 0.3
tiny_eps = 1e-08
highest = lax.Precision.HIGHEST
f32 = jnp.float32


def exchange(blocks, axis):
    return lax.all_to_all(blocks, axis, 0, 0, axis_index_groups=[order(axis)])


def order(axis):
    count = lax.axis_size(axis)
    if axis == "tensor":
        planes = count // 2
        others = sorted(range(planes - 1), key=lambda z: (min(z, planes - z), -z))
        return [2 * z + core for z in [planes - 1] + others for core in (1, 0)]
    side = math.isqrt(count)
    turned = [(i + 4) % side for i in range(side)]
    return [side * y + x for y in turned for x in turned]


def copies(block, axis):
    return jnp.broadcast_to(block[None], (lax.axis_size(axis),) + block.shape)


def eliminate(blocks, size, width):
    sublane = lax.broadcasted_iota(jnp.int32, (8, width), 0)

    def spread_row(block, row):
        return jnp.broadcast_to(block[row:row + 1, :], (8, width))

    def spread_column(block, column):
        return jnp.broadcast_to(block[:, column:column + 1], (8, width))

    count = size // 8
    for first in range(count):
        live = range(first, count)
        columns = [{i: spread_column(blocks[i], 8 * first + k) for i in live} for k in range(8)]
        for k in range(8):
            inverse = 1.0 / spread_row(columns[k][first], k)
            row = spread_row(blocks[first], k)
            ratio = {i: columns[k][i] * inverse for i in live}
            below = jnp.where(sublane > k, ratio[first], 0.0)
            for later in range(k + 1, 8):
                entry = spread_row(columns[later][first], k)
                for i in live:
                    if i == first and later == k + 1:
                        step = (columns[k][i] * entry) * inverse
                    else:
                        step = ratio[i] * entry
                    columns[later][i] = columns[later][i] - step
            if k < 7:
                blocks[first] = blocks[first] - below * row
            for i in range(first + 1, count):
                blocks[i] = blocks[i] - ratio[i] * row
    return blocks


def dot(a, b, contract=((1,), (0,)), precision=highest):
    return lax.dot_general(a, b, (contract, ((), ())), precision=precision, preferred_element_type=f32)


def terms(x, count):
    parts = []
    for _ in range(count):
        parts.append(x.astype(jnp.bfloat16))
        x = x - parts[-1].astype(f32)
    return parts


def stacked(a, b, depth):
    a, b = terms(a, depth), terms(b, depth)
    pairs = [(i, j) for i in range(depth) for j in range(depth) if i + j < depth]
    return dot(
        jnp.concatenate([a[i] for i, _ in pairs], axis=1),
        jnp.concatenate([b[j] for _, j in pairs], axis=0),
        precision=lax.Precision.DEFAULT,
    )


def left_kernel(buffer_ref, basis_ref, copies_ref):
    buffer, basis = terms(buffer_ref[...], 3), terms(basis_ref[...], 3)
    pairs = [(i, j) for i in range(3) for j in range(3) if i + j < 3]
    part = dot(
        jnp.concatenate([buffer[i] for i, _ in pairs], axis=1),
        jnp.concatenate([basis[j] for _, j in pairs], axis=1),
        ((1,), (1,)),
        lax.Precision.DEFAULT,
    )
    half = part.shape[0] // 2
    packed = jnp.concatenate([part[:half], part[half:]], axis=1)
    copies_ref[...] = jnp.broadcast_to(packed[None], copies_ref.shape)


def product_kernel(parts_ref, buffer_ref, left_ref, products_ref):
    rank = left_ref.shape[1]
    packed = jnp.sum(parts_ref[...], axis=0)
    left = jnp.concatenate([packed[:, :rank], packed[:, rank:]], axis=0)
    left_ref[...] = left
    padded = jnp.concatenate([left, jnp.zeros((left.shape[0], 128 - rank), f32)], axis=1)
    products = stacked(left.T, jnp.concatenate([buffer_ref[...], padded], axis=1), 3)
    slabs = [products[:, i:i + 128] for i in range(0, products.shape[1], 128)]
    products_ref[...] = jnp.swapaxes(jnp.stack(slabs, axis=0), 0, 1)


def factor_kernel(whole_ref, left_ref, right_ref, ortho_ref, copies_ref):
    rank = left_ref.shape[1]
    slabs = right_ref.shape[1] // 128
    row = lax.broadcasted_iota(jnp.int32, (rank, 2 * rank), 0)
    column = lax.broadcasted_iota(jnp.int32, (rank, 2 * rank), 1)
    start = jnp.where(column < rank, whole_ref[:, slabs, :], jnp.where(column == row + rank, 1.0, 0.0))
    blocks = eliminate([start[8 * i:8 * i + 8] for i in range(rank // 8)], rank, 2 * rank)
    done = jnp.concatenate(blocks, axis=0)
    pivots = jnp.sum(jnp.where(row == column, done, 0.0), axis=1, keepdims=True)
    inverse = (done / jnp.sqrt(pivots))[:, rank:]
    right = stacked(inverse, jnp.concatenate([whole_ref[:, i, :] for i in range(slabs)], axis=1), 3)
    right_ref[...] = right
    total = sum(right[:, 128 * i:128 * i + 128] * right[:, 128 * i:128 * i + 128] for i in range(slabs))
    squares = dot(jnp.ones((8, 128), f32), total, ((1,), (1,)))[:1]
    squares = jnp.concatenate([squares, jnp.zeros((1, 128 - rank), f32)], axis=1)
    copies_ref[...] = jnp.broadcast_to(squares[None], copies_ref.shape)
    ortho_ref[...] = dot(left_ref[...], inverse, ((1,), (1,)))


def update_kernel(factor, squares_ref, right_ref, ortho_ref, buffer_ref, weight_ref,
                  new_weight_ref, new_momentum_ref, new_basis_ref):
    rows, rank = ortho_ref.shape
    norms = jnp.sqrt(jnp.sum(squares_ref[...], axis=0))[:, :rank]
    scale = 1.0 / (norms + tiny_eps)
    row = lax.broadcasted_iota(jnp.int32, (rank, rank), 0)
    column = lax.broadcasted_iota(jnp.int32, (rank, rank), 1)
    turned = jnp.sum(jnp.where(row == column, scale, 0.0), axis=1, keepdims=True)
    right = right_ref[...]
    ortho = ortho_ref[...]
    both = jnp.concatenate([(1.0 - decay_rate) * ortho, factor * (ortho * scale)], axis=0)
    update = stacked(both, right, 2)
    new_momentum_ref[...] = buffer_ref[...] - update[:rows]
    new_weight_ref[...] = weight_ref[...] - update[rows:]
    new_basis_ref[...] = right * turned


def call(kernel, name, args, shapes):
    in_vmem = pl.BlockSpec(memory_space=pltpu.VMEM)
    return pl.pallas_call(
        kernel,
        out_shape=[jax.ShapeDtypeStruct(shape, f32) for shape in shapes],
        in_specs=[in_vmem] * len(args),
        out_specs=[in_vmem] * len(shapes),
        compiler_params=pltpu.CompilerParams(vmem_limit_bytes=16 * 2**20),
        name=name,
    )(*args)


def per_device(weight, momentum, gradient, right_basis):
    rank = right_basis.shape[1]
    rows, cols = weight.shape
    fsdp, tensor = lax.axis_size("fsdp"), lax.axis_size("tensor")
    buffer = momentum + gradient.astype(f32)
    (parts,) = call(left_kernel, "left", (buffer, right_basis.T), [(tensor, rows // 2, 2 * rank)])
    parts = exchange(parts, "tensor")
    left, products = call(product_kernel, "products", (parts, buffer), [(rows, rank), (rank, 8, 128)])
    mine = jnp.sum(exchange(products, "fsdp"), axis=0)
    whole = exchange(copies(mine, "fsdp"), "fsdp")
    right, ortho, squares = call(
        factor_kernel, "factor", (whole, left),
        [(rank, cols), (rows, rank), (tensor, 1, 128)])
    squares = exchange(squares, "tensor")
    factor = step_size * math.sqrt(rows * fsdp * cols * tensor / rank)
    new_weight, new_momentum, new_basis = call(
        functools.partial(update_kernel, factor), "update", (squares, right, ortho, buffer, weight),
        [(rows, cols), (rows, cols), (rank, cols)])
    return (new_weight, new_momentum, new_basis.T)


def solution(mesh):
    placed = (P("fsdp", "tensor"), P("fsdp", "tensor"), P("fsdp", "tensor"), P("tensor", None))
    return jax.shard_map(
        per_device,
        mesh=mesh,
        in_specs=placed,
        out_specs=(P("fsdp", "tensor"), P("fsdp", "tensor"), P("tensor", None)),
        check_vma=False,
    )
```

```python
import functools
import math

import jax
import jax.numpy as jnp
from jax import lax
from jax.experimental import pallas as pl
from jax.experimental.pallas import tpu as pltpu
from jax.sharding import PartitionSpec as P

decay_rate = 0.95
step_size = 0.3
tiny_eps = 1e-08
highest = lax.Precision.HIGHEST
f32 = jnp.float32


def exchange(blocks, axis):
    return lax.all_to_all(blocks, axis, 0, 0, axis_index_groups=[order(axis)])


def order(axis):
    count = lax.axis_size(axis)
    if axis == "tensor":
        planes = count // 2
        others = sorted(range(planes - 1), key=lambda z: (min(z, planes - z), -z))
        return [2 * z + core for z in [planes - 1] + others for core in (1, 0)]
    side = math.isqrt(count)
    middle = side // 2
    turned = sorted(range(side), key=lambda i: (abs(i - middle), i))
    return [side * y + x for y in turned for x in turned]


def copies(block, axis):
    return jnp.broadcast_to(block[None], (lax.axis_size(axis),) + block.shape)


def eliminate(blocks, size, width):
    sublane = lax.broadcasted_iota(jnp.int32, (8, width), 0)

    def spread_row(block, row):
        return jnp.broadcast_to(block[row:row + 1, :], (8, width))

    def spread_column(block, column):
        return jnp.broadcast_to(block[:, column:column + 1], (8, width))

    count = size // 8
    for first in range(count):
        live = range(first, count)
        columns = [{i: spread_column(blocks[i], 8 * first + k) for i in live} for k in range(8)]
        for k in range(8):
            inverse = 1.0 / spread_row(columns[k][first], k)
            row = spread_row(blocks[first], k)
            ratio = {i: columns[k][i] * inverse for i in live}
            below = jnp.where(sublane > k, ratio[first], 0.0)
            for later in range(k + 1, 8):
                entry = spread_row(columns[later][first], k)
                for i in live:
                    if i == first and later == k + 1:
                        step = (columns[k][i] * entry) * inverse
                    else:
                        step = ratio[i] * entry
                    columns[later][i] = columns[later][i] - step
            if k < 7:
                blocks[first] = blocks[first] - below * row
            for i in range(first + 1, count):
                blocks[i] = blocks[i] - ratio[i] * row
    return blocks


def dot(a, b, contract=((1,), (0,)), precision=highest):
    return lax.dot_general(a, b, (contract, ((), ())), precision=precision, preferred_element_type=f32)


def terms(x, count):
    parts = []
    for _ in range(count):
        parts.append(x.astype(jnp.bfloat16))
        x = x - parts[-1].astype(f32)
    return parts


def stacked(a, b, depth):
    a, b = terms(a, depth), terms(b, depth)
    pairs = [(i, j) for i in range(depth) for j in range(depth) if i + j < depth]
    return dot(
        jnp.concatenate([a[i] for i, _ in pairs], axis=1),
        jnp.concatenate([b[j] for _, j in pairs], axis=0),
        precision=lax.Precision.DEFAULT,
    )


def left_kernel(buffer_ref, basis_ref, copies_ref):
    buffer, basis = terms(buffer_ref[...], 3), terms(basis_ref[...], 3)
    pairs = [(i, j) for i in range(3) for j in range(3) if i + j < 3]
    part = dot(
        jnp.concatenate([buffer[i] for i, _ in pairs], axis=1),
        jnp.concatenate([basis[j] for _, j in pairs], axis=1),
        ((1,), (1,)),
        lax.Precision.DEFAULT,
    )
    half = part.shape[0] // 2
    packed = jnp.concatenate([part[:half], part[half:]], axis=1)
    copies_ref[...] = jnp.broadcast_to(packed[None], copies_ref.shape)


def product_kernel(parts_ref, buffer_ref, left_ref, products_ref):
    rank = left_ref.shape[1]
    packed = jnp.sum(parts_ref[...], axis=0)
    left = jnp.concatenate([packed[:, :rank], packed[:, rank:]], axis=0)
    left_ref[...] = left
    padded = jnp.concatenate([left, jnp.zeros((left.shape[0], 128 - rank), f32)], axis=1)
    products = stacked(left.T, jnp.concatenate([buffer_ref[...], padded], axis=1), 3)
    slabs = [products[:, i:i + 128] for i in range(0, products.shape[1], 128)]
    products_ref[...] = jnp.swapaxes(jnp.stack(slabs, axis=0), 0, 1)


def factor_kernel(whole_ref, left_ref, right_ref, ortho_ref, copies_ref):
    rank = left_ref.shape[1]
    slabs = right_ref.shape[1] // 128
    row = lax.broadcasted_iota(jnp.int32, (rank, 2 * rank), 0)
    column = lax.broadcasted_iota(jnp.int32, (rank, 2 * rank), 1)
    start = jnp.where(column < rank, whole_ref[:, slabs, :], jnp.where(column == row + rank, 1.0, 0.0))
    blocks = eliminate([start[8 * i:8 * i + 8] for i in range(rank // 8)], rank, 2 * rank)
    done = jnp.concatenate(blocks, axis=0)
    pivots = jnp.sum(jnp.where(row == column, done, 0.0), axis=1, keepdims=True)
    inverse = (done / jnp.sqrt(pivots))[:, rank:]
    right = stacked(inverse, jnp.concatenate([whole_ref[:, i, :] for i in range(slabs)], axis=1), 3)
    right_ref[...] = right
    total = sum(right[:, 128 * i:128 * i + 128] * right[:, 128 * i:128 * i + 128] for i in range(slabs))
    squares = dot(jnp.ones((8, 128), f32), total, ((1,), (1,)))[:1]
    squares = jnp.concatenate([squares, jnp.zeros((1, 128 - rank), f32)], axis=1)
    copies_ref[...] = jnp.broadcast_to(squares[None], copies_ref.shape)
    ortho_ref[...] = dot(left_ref[...], inverse, ((1,), (1,)))


def update_kernel(factor, squares_ref, right_ref, ortho_ref, buffer_ref, weight_ref,
                  new_weight_ref, new_momentum_ref, new_basis_ref):
    rows, rank = ortho_ref.shape
    norms = jnp.sqrt(jnp.sum(squares_ref[...], axis=0))[:, :rank]
    scale = 1.0 / (norms + tiny_eps)
    row = lax.broadcasted_iota(jnp.int32, (rank, rank), 0)
    column = lax.broadcasted_iota(jnp.int32, (rank, rank), 1)
    turned = jnp.sum(jnp.where(row == column, scale, 0.0), axis=1, keepdims=True)
    right = right_ref[...]
    ortho = ortho_ref[...]
    both = jnp.concatenate([(1.0 - decay_rate) * ortho, factor * (ortho * scale)], axis=0)
    update = stacked(both, right, 2)
    new_momentum_ref[...] = buffer_ref[...] - update[:rows]
    new_weight_ref[...] = weight_ref[...] - update[rows:]
    new_basis_ref[...] = right * turned


def call(kernel, name, args, shapes):
    in_vmem = pl.BlockSpec(memory_space=pltpu.VMEM)
    return pl.pallas_call(
        kernel,
        out_shape=[jax.ShapeDtypeStruct(shape, f32) for shape in shapes],
        in_specs=[in_vmem] * len(args),
        out_specs=[in_vmem] * len(shapes),
        compiler_params=pltpu.CompilerParams(vmem_limit_bytes=16 * 2**20),
        name=name,
    )(*args)


def per_device(weight, momentum, gradient, right_basis):
    rank = right_basis.shape[1]
    rows, cols = weight.shape
    fsdp, tensor = lax.axis_size("fsdp"), lax.axis_size("tensor")
    buffer = momentum + gradient.astype(f32)
    (parts,) = call(left_kernel, "left", (buffer, right_basis.T), [(tensor, rows // 2, 2 * rank)])
    parts = exchange(parts, "tensor")
    left, products = call(product_kernel, "products", (parts, buffer), [(rows, rank), (rank, 8, 128)])
    mine = jnp.sum(exchange(products, "fsdp"), axis=0)
    whole = exchange(copies(mine, "fsdp"), "fsdp")
    right, ortho, squares = call(
        factor_kernel, "factor", (whole, left),
        [(rank, cols), (rows, rank), (tensor, 1, 128)])
    squares = exchange(squares, "tensor")
    factor = step_size * math.sqrt(rows * fsdp * cols * tensor / rank)
    new_weight, new_momentum, new_basis = call(
        functools.partial(update_kernel, factor), "update", (squares, right, ortho, buffer, weight),
        [(rows, cols), (rows, cols), (rank, cols)])
    return (new_weight, new_momentum, new_basis.T)


def solution(mesh):
    placed = (P("fsdp", "tensor"), P("fsdp", "tensor"), P("fsdp", "tensor"), P("tensor", None))
    return jax.shard_map(
        per_device,
        mesh=mesh,
        in_specs=placed,
        out_specs=(P("fsdp", "tensor"), P("fsdp", "tensor"), P("tensor", None)),
        check_vma=False,
    )
```
